256 devices in a mesh: outer: 8 (over z), inner: 32 (over x, y, core).
Axes of the slice: x: 4, y: 4, z: 8, core: 2. Of those that a mesh axis runs over, the one named last changes fastest.
Arguments:
- resid: bfloat16 [32768, 4096], P(('outer', 'inner')), may hold values from -30 to 30, as said below
- query_mr: bfloat16 [32768, 4096], P(('outer', 'inner')), may hold values from -6 to 6
- key_mr: bfloat16 [32768, 4096], P(('outer', 'inner')), may hold values from -6 to 6
- value_mr: bfloat16 [32768, 4096], P(('outer', 'inner')), may hold values from -6 to 6
- query_li: bfloat16 [32768, 4096], P(('outer', 'inner')), may hold values from -6 to 6
- key_li: bfloat16 [32768, 4096], P(('outer', 'inner')), may hold values from -6 to 6
- mr_filter: bfloat16 [128, 256], replicated, may hold values from -0.5 to 0.5
- pole_rate: float32 [16, 256], replicated, may hold values from 6.1035155e-07 to 0.05
- residue: float32 [16, 256], replicated, may hold values from -2.1 to 2.1
Outputs:
- mixed_mr: bfloat16 [32768, 4096], P(('outer', 'inner'))
- long_out: bfloat16 [32768, 4096], P(('outer', 'inner'))
The draws below stay inside these ranges and needn't reach their ends.
Inputs may be any that keep to these rules, and one draw needn't show every extreme that they name: `resid`: activations of the residual stream.
All inputs are finite; a program needn't handle non-finite values.
Results may differ from the reference program's by a relative error of at most 0.006.
Values may be sent and summed in bfloat16 or wider, within the bound.
No kernel may reach another device: no remote copies, remote signals or barrier semaphores. Data moves between devices by JAX's collectives and lax.ppermute only.
A program may use at most 256 MiB of HBM per device.

```python
import math
import jax
import jax.numpy as jnp
from jax import lax

D = 4096
GROUPS = 256
MR_LEN = 128
POLES = 16
TOK_DEV = 128
TOKENS = 32768


def draw_resid(key, part):
    key_entries, key_row, key_col = jax.random.split(key, 3)
    row_scale = jnp.exp(jax.random.uniform(key_row, (TOKENS, 1), jnp.float32, jnp.log(0.3), jnp.log(3.0)))
    col_scale = jnp.exp(jax.random.uniform(key_col, (1, D), jnp.float32, jnp.log(0.5), jnp.log(2.5)))
    entries = jnp.clip(jax.random.normal(key_entries, (TOKENS, D), jnp.float32), -4.0, 4.0)
    return (entries * row_scale * col_scale).astype(jnp.bfloat16)


def levels(rng, extent, cuts, least, largest):
    gain, own = 1.0, jax.random.fold_in(rng, 6)
    for position, shards_of in cuts:
        draws = jnp.exp(jax.random.uniform(jax.random.fold_in(own, position), (shards_of,), jnp.float32, least / len(cuts), largest / len(cuts)))
        gain = gain * jnp.repeat(draws, extent[position] // shards_of).reshape([-1 if axis == position else 1 for axis in range(len(extent))])
    return gain


def centred(rng, shape, deviation, bound, shards=(), kind=jnp.bfloat16):
    result = deviation * jax.random.normal(rng, shape, jnp.float32)
    if shards:
        result = result * levels(rng, shape, shards, -0.22, 0.18)
    return jnp.clip(result, -bound, bound).astype(kind)


def setup_inputs(seed: int = 0) -> dict:
    arg_keys = jax.random.split(jax.random.key(seed), 10)
    resid = draw_resid(jax.random.fold_in(arg_keys[9], 71), 0)
    query_mr = centred(arg_keys[1], (TOKENS, D), 1.0, 6.0, ((0, 256),))
    key_mr = centred(arg_keys[2], (TOKENS, D), 1.0, 6.0, ((0, 256),))
    value_mr = centred(arg_keys[3], (TOKENS, D), 1.0, 6.0, ((0, 256),))
    query_li = centred(arg_keys[4], (TOKENS, D), 1.0, 6.0, ((0, 256),))
    key_li = centred(arg_keys[5], (TOKENS, D), 1.0, 6.0, ((0, 256),))
    mr_filter = centred(arg_keys[6], (MR_LEN, GROUPS), MR_LEN ** -0.5, 0.5)
    pole_rate = jnp.clip(jnp.exp(jax.random.uniform(arg_keys[7], (POLES, GROUPS), jnp.float32, math.log(6.103515488575795e-07), math.log(0.05))), 6.103515488575795e-07, 0.05)
    residue = centred(arg_keys[8], (POLES, GROUPS), 0.35, 2.1, (), jnp.float32)
    return {"resid": resid, "query_mr": query_mr, "key_mr": key_mr, "value_mr": value_mr, "query_li": query_li, "key_li": key_li, "mr_filter": mr_filter, "pole_rate": pole_rate, "residue": residue}


EPSILON = 1e-06
HIGHEST = lax.Precision.HIGHEST

def toeplitz_index(count_rows, count_cols, offset, length):
    lag_table = jnp.arange(count_rows, dtype=jnp.int32)[:, None] + offset - jnp.arange(count_cols, dtype=jnp.int32)[None, :]
    inside = (lag_table >= 0) & (lag_table < length)
    return (jnp.clip(lag_table, 0, length - 1).astype(jnp.int32), inside)

def medium_block(extended, filter_taps):
    tap_count, group_count = filter_taps.shape
    row_count = extended.shape[0] - tap_count + 1
    lag_index, inside = toeplitz_index(row_count, extended.shape[0], tap_count - 1, tap_count)
    toeplitz = jnp.where(inside[:, :, None], jnp.take(filter_taps, lag_index, axis=0), jnp.zeros((), filter_taps.dtype))
    grouped = extended.reshape(extended.shape[0], group_count, -1)
    mixed = jnp.einsum('tsg,sgc->tgc', toeplitz.astype(jnp.float32), grouped.astype(jnp.float32))
    return mixed.reshape(row_count, -1)

def modal_tables(pole_rate, residue, row_count):
    scaled = residue * jnp.sqrt(-jnp.expm1(-2.0 * pole_rate))
    positions = jnp.arange(row_count, dtype=jnp.float32)
    powers = jnp.exp(-pole_rate[None] * positions[:, None, None])
    kernel = lax.optimization_barrier(jnp.sum(powers * scaled[None], axis=1))
    ending = jnp.exp(-pole_rate[None] * (row_count - 1.0 - positions)[:, None, None])
    entering = powers * (jnp.exp(-pole_rate) * scaled)[None]
    block_decay = jnp.exp(-pole_rate * row_count)
    return (kernel, ending, entering, block_decay)

def long_block(inputs_bf, state_in, kernel, ending, entering, group_count):
    row_count = inputs_bf.shape[0]
    lag_index, inside = toeplitz_index(row_count, row_count, 0, row_count)
    toeplitz = jnp.where(inside[:, :, None], jnp.take(kernel, lag_index, axis=0), 0.0)
    grouped = inputs_bf.astype(jnp.float32).reshape(row_count, group_count, -1)
    local_part = jnp.einsum('tsg,sgc->tgc', toeplitz, grouped, precision=HIGHEST)
    carried = jnp.einsum('tpg,pgc->tgc', entering, state_in, precision=HIGHEST)
    block_state = jnp.einsum('spg,sgc->pgc', ending, grouped, precision=HIGHEST)
    return ((local_part + carried).reshape(row_count, -1), block_state)

def reference(resid, query_mr, key_mr, value_mr, query_li, key_li, mr_filter, pole_rate, residue):
    tap_count = mr_filter.shape[0]
    group_count = mr_filter.shape[1]
    product = (key_mr.astype(jnp.float32) * value_mr.astype(jnp.float32)).astype(jnp.bfloat16)
    padded = jnp.concatenate([jnp.zeros((tap_count - 1, D), jnp.bfloat16), product], axis=0)

    def medium_step(block_index):
        row_start = (block_index * TOK_DEV).astype(jnp.int32)
        extended = lax.dynamic_slice_in_dim(padded, row_start, TOK_DEV + tap_count - 1, 0)
        return medium_block(extended, mr_filter)
    convolved = lax.map(medium_step, jnp.arange(TOKENS // TOK_DEV, dtype=jnp.int32)).reshape(TOKENS, D)
    mixed_mr = (resid.astype(jnp.float32) + query_mr.astype(jnp.float32) * convolved).astype(jnp.bfloat16)
    stream = mixed_mr.astype(jnp.float32)
    inverse_rms = lax.rsqrt(lax.optimization_barrier(jnp.mean(stream * stream, axis=1, keepdims=True)) + EPSILON)
    gated = (key_li.astype(jnp.float32) * stream * inverse_rms).astype(jnp.bfloat16)
    kernel, ending, entering, block_decay = modal_tables(pole_rate, residue, TOK_DEV)
    blocks = gated.reshape(TOKENS // TOK_DEV, TOK_DEV, D)

    def long_step(state_in, block_rows):
        filtered, block_state = long_block(block_rows, state_in, kernel, ending, entering, group_count)
        return (block_decay[:, :, None] * state_in + block_state, filtered)
    zero_state = jnp.zeros((POLES, group_count, D // group_count), jnp.float32)
    final_state, filtered = lax.scan(long_step, zero_state, blocks)
    filtered = filtered.reshape(TOKENS, D)
    long_out = (query_li.astype(jnp.float32) * filtered).astype(jnp.bfloat16)
    return (mixed_mr, long_out)
```

```python
import functools

import jax
import jax.numpy as jnp
from jax import lax
from jax.experimental import pallas as pl
from jax.experimental.pallas import tpu as pltpu
from jax.sharding import PartitionSpec as P

EPSILON = 1e-06
AXES = ("outer", "inner")
LANES = 128
HALF = LANES // 2
SUB = 32
PARTS = 4
LARGE = 58 * 1024 * 1024
SMALL = 4 * 1024 * 1024
F32 = jnp.float32
BF16 = jnp.bfloat16
VMEM = pl.BlockSpec(memory_space=pltpu.VMEM)
HBM = pl.BlockSpec(memory_space=pltpu.HBM)
SMEM = pl.BlockSpec(memory_space=pltpu.SMEM)


def from_behind(block, axis, distance):
    devices = range(lax.axis_size(axis))
    route = [(i - distance, i) for i in devices if i - distance in devices]
    return lax.ppermute(block, axis, route)


def span(index, size):
    return pl.ds(pl.multiple_of(index * size, size), size)


def own_lanes(stack, rows, groups, per_group):
    group = lax.broadcasted_iota(jnp.int32, (rows, LANES), 1) % (groups * per_group) // per_group
    out = stack[:rows]
    for g in range(1, groups):
        out = jnp.where(group == g, stack[g * rows : (g + 1) * rows], out)
    return out


def half_turn(block):
    return jnp.concatenate([block[:, HALF:], block[:, :HALF]], axis=1)


def causal(table, old, new, per_group):
    rows = new.shape[0]

    def window(before, now, b):
        return jnp.concatenate([before[b * SUB :], now[: (b + 1) * SUB]], axis=0)

    old_turned, new_turned = half_turn(old), half_turn(new)
    depth = rows + SUB
    low = lax.broadcasted_iota(jnp.int32, (depth, LANES), 1) < HALF
    first, second = [], []
    for b in range(0, rows // SUB, 2):
        straight, turned = window(old, new, b), window(old_turned, new_turned, b + 1)
        first.append(jnp.where(low, straight, turned))
        second.append(jnp.where(low, turned, straight))
    middle = table.shape[0] // 2
    stack_a = jnp.dot(table[:middle], jnp.concatenate(first, axis=1), preferred_element_type=F32)
    stack_b = jnp.dot(table[middle:], jnp.concatenate(second, axis=1), preferred_element_type=F32)
    low = lax.broadcasted_iota(jnp.int32, (SUB, LANES), 1) < HALF
    out = []
    for j in range(rows // SUB // 2):
        cols = slice(j * LANES, (j + 1) * LANES)
        a = own_lanes(stack_a[:, cols], SUB, HALF // per_group, per_group)
        b = own_lanes(stack_b[:, cols], SUB, HALF // per_group, per_group)
        out.append(jnp.where(low, a, b))
        out.append(pltpu.roll(jnp.where(low, b, a), HALF, 1))
    return out


def table_kernel(per_group, medium_taps_ref, long_taps_ref, medium_hbm, long_hbm, medium_ref, long_ref, sems):
    groups = LANES // per_group
    slabs = medium_ref.shape[0]
    row = lax.broadcasted_iota(jnp.int32, (SUB, LANES), 0)
    lane = lax.broadcasted_iota(jnp.int32, (SUB, LANES), 1)
    copies = []
    for i, (taps_ref, table_ref, out_hbm) in enumerate(
        ((medium_taps_ref, medium_ref, medium_hbm), (long_taps_ref, long_ref, long_hbm))
    ):

        def fill(slab, _):
            taps = taps_ref[span(slab, groups), :]
            for g in range(groups):
                turned = pltpu.roll(jnp.broadcast_to(taps[g : g + 1, :], (SUB, LANES)), 0, 1, stride=1, stride_axis=0)
                rows = slice(g * SUB, (g + 1) * SUB)
                table_ref[slab, rows, :LANES] = jnp.where(lane > row, turned, 0.0).astype(BF16)
                table_ref[slab, rows, LANES:] = jnp.where(lane <= row, turned, 0.0)[:, :SUB].astype(BF16)
            return 0

        lax.fori_loop(0, slabs, fill, 0, unroll=4)
        copies.append(pltpu.make_async_copy(table_ref, out_hbm, sems.at[i]))
        copies[i].start()
    for copy in copies:
        copy.wait()


def medium_kernel(per_group, table_hbm, rim_hbm, product_hbm, query_hbm, resid_hbm, key_hbm, ending_hbm, long_hbm,
                  entering_hbm, mixed_hbm, gated_hbm, state_ref, table_ref, rim_ref, product_ref, query_ref, resid_ref,
                  key_ref, ending_ref, mixed_ref, gated_ref, square_ref, load_sems, late_sems, store_sems):
    rows, width = product_ref.shape
    slabs = width // LANES // PARTS

    def loads(part):
        cols = span(part, width // PARTS)
        several = pl.ds(part * slabs, slabs)
        pairs = [(table_hbm.at[several], table_ref.at[several])]
        pairs += [
            (source.at[:, cols], target.at[:, cols])
            for source, target in (
                (rim_hbm, rim_ref), (product_hbm, product_ref), (query_hbm, query_ref), (resid_hbm, resid_ref)
            )
        ]
        return [pltpu.make_async_copy(*pair, load_sems.at[part, i]) for i, pair in enumerate(pairs)]

    def store(source, target, part, which):
        cols = span(part, width // PARTS)
        return pltpu.make_async_copy(source.at[:, cols], target.at[:, cols], store_sems.at[which, part])

    late = [
        pltpu.make_async_copy(key_hbm, key_ref, late_sems.at[0]),
        pltpu.make_async_copy(ending_hbm, ending_ref, late_sems.at[1]),
    ]
    for part in range(PARTS):
        for copy in loads(part):
            copy.start()
    for copy in late:
        copy.start()
    square_ref[...] = jnp.zeros_like(square_ref)

    def mix(part, _):
        for copy in loads(part):
            copy.wait()

        def one(turn, _):
            slab = part * slabs + turn
            cols = span(slab, LANES)
            convolved = causal(table_ref[slab], rim_ref[:, cols], product_ref[:, cols], per_group)
            for b, sums in enumerate(convolved):
                block = slice(b * SUB, (b + 1) * SUB)
                mixed = (resid_ref[block, cols].astype(F32) + query_ref[block, cols].astype(F32) * sums).astype(BF16)
                mixed_ref[block, cols] = mixed
                stream = mixed.astype(F32)
                square_ref[block, :] += stream * stream
            return 0

        lax.fori_loop(0, slabs, one, 0, unroll=True)
        store(mixed_ref, mixed_hbm, part, 0).start()
        return 0

    lax.fori_loop(0, PARTS, mix, 0)
    mean = jnp.sum(square_ref[...], axis=1, keepdims=True) * (1.0 / width)
    square_ref[...] = jnp.broadcast_to(lax.rsqrt(mean + EPSILON), square_ref.shape)
    owners, poles, owned = state_ref.shape
    for copy in late:
        copy.wait()

    def gate(part, _):
        def one(turn, _):
            slab = part * slabs + turn
            cols = span(slab, LANES)
            gated = (key_ref[:, cols].astype(F32) * mixed_ref[:, cols].astype(F32) * square_ref[...]).astype(BF16)
            gated_ref[:, cols] = gated
            stack = jnp.dot(ending_ref[cols, :], gated, preferred_element_type=F32)
            state_ref[slab] = own_lanes(stack, poles, LANES // per_group, per_group).astype(BF16)
            return 0

        lax.fori_loop(0, slabs, one, 0, unroll=True)
        store(gated_ref, gated_hbm, part, 1).start()
        return 0

    lax.fori_loop(0, PARTS, gate, 0)
    for part in range(PARTS):
        store(mixed_ref, mixed_hbm, part, 0).wait()
        store(gated_ref, gated_hbm, part, 1).wait()


def local_kernel(per_group, table_hbm, gated_hbm, after_ref, local_hbm, token_ref, table_ref, gated_ref, local_ref,
                 load_sems, store_sems):
    rows, width = gated_ref.shape
    slabs = width // LANES // PARTS

    def loads(part):
        cols = span(part, width // PARTS)
        several = pl.ds(part * slabs, slabs)
        return [
            pltpu.make_async_copy(table_hbm.at[several], table_ref.at[several], load_sems.at[part, 0]),
            pltpu.make_async_copy(gated_hbm.at[:, cols], gated_ref.at[:, cols], load_sems.at[part, 1]),
        ]

    def store(part):
        cols = span(part, width // PARTS)
        return pltpu.make_async_copy(local_ref.at[:, cols], local_hbm.at[:, cols], store_sems.at[part])

    for part in range(PARTS):
        for copy in loads(part):
            copy.start()
    token_ref[...] = jnp.zeros_like(token_ref)

    def convolve(part, _):
        for copy in loads(part):
            copy.wait()

        def one(turn, _):
            slab = part * slabs + turn
            cols = span(slab, LANES)
            old = jnp.zeros((rows, LANES), BF16)
            for b, sums in enumerate(causal(table_ref[slab], old, gated_ref[:, cols], per_group)):
                local_ref[b * SUB : (b + 1) * SUB, cols] = sums
            return 0

        lax.fori_loop(0, slabs, one, 0, unroll=True)
        store(part).start()
        return 0

    lax.fori_loop(0, PARTS, convolve, 0)
    for part in range(PARTS):
        store(part).wait()


def total_kernel(states_ref, decay_ref, total_ref):
    decay = decay_ref[...]
    total = states_ref[0].astype(F32)
    for i in range(1, states_ref.shape[0]):
        total = decay * total + states_ref[i].astype(F32)
    total = total.astype(BF16)
    for i in range(total_ref.shape[0]):
        total_ref[i] = total


def enter_kernel(place_ref, states_ref, totals_ref, decay_ref, group_decay_ref, after_ref, entered_ref):
    place = place_ref[0]
    group_decay = group_decay_ref[...]

    def one(turn, state):
        return group_decay * state + totals_ref[turn].astype(F32)

    state = lax.fori_loop(0, place, one, jnp.zeros_like(group_decay))
    decay = decay_ref[...]
    for i in range(states_ref.shape[0]):
        entered_ref[i] = state.astype(BF16)
        if i + 1 < states_ref.shape[0]:
            state = decay * state + states_ref[i].astype(F32)


def final_kernel(per_group, entering_hbm, state_ref, local_hbm, query_hbm, out_hbm,
                 entering_ref, local_ref, query_ref, out_ref, load_sems, store_sems):
    owners, poles, owned = state_ref.shape
    width = owners * owned
    pair = 2
    steps = owners // pair // PARTS

    def loads(part):
        cols = span(part, width // PARTS)
        pairs = ((entering_hbm, entering_ref), (local_hbm, local_ref), (query_hbm, query_ref))
        return [
            pltpu.make_async_copy(source.at[:, cols], target.at[:, cols], load_sems.at[part, i])
            for i, (source, target) in enumerate(pairs)
        ]

    def store(part):
        cols = span(part, width // PARTS)
        return pltpu.make_async_copy(out_ref.at[:, cols], out_hbm.at[:, cols], store_sems.at[part])

    for part in range(PARTS):
        for copy in loads(part):
            copy.start()
    spread = pair * owned // per_group
    row_group = lax.broadcasted_iota(jnp.int32, (spread * poles, pair * owned), 0) // poles
    lane_group = lax.broadcasted_iota(jnp.int32, (spread * poles, pair * owned), 1) // per_group
    own = row_group == lane_group

    def finish(part, _):
        for copy in loads(part):
            copy.wait()

        def one(turn, _):
            slab = part * steps + turn
            cols = span(slab, pair * owned)
            state = jnp.concatenate([state_ref[slab * pair + i] for i in range(pair)], axis=1)
            diagonal = jnp.where(own, jnp.concatenate([state] * spread, axis=0), jnp.zeros((), BF16))
            carried = jnp.dot(entering_ref[:, cols], diagonal, preferred_element_type=F32)
            out_ref[:, cols] = (query_ref[:, cols].astype(F32) * (local_ref[:, cols] + carried)).astype(BF16)
            return 0

        lax.fori_loop(0, steps, one, 0, unroll=True)
        store(part).start()
        return 0

    lax.fori_loop(0, PARTS, finish, 0)
    for part in range(PARTS):
        store(part).wait()


def call(body, out, in_specs, out_specs, name, scratch=(), flops=0, moved=0, limit=LARGE):
    return pl.pallas_call(
        body,
        out_shape=out,
        in_specs=in_specs,
        out_specs=out_specs,
        scratch_shapes=scratch,
        name=name,
        cost_estimate=pl.CostEstimate(flops=flops, bytes_accessed=moved, transcendentals=0),
        compiler_params=pltpu.CompilerParams(vmem_limit_bytes=limit),
    )


def shards(resid, query_mr, key_mr, value_mr, query_li, key_li, mr_filter, pole_rate, residue):
    tap_count, group_count = mr_filter.shape
    poles = pole_rate.shape[0]
    rows, width = resid.shape
    per_group = width // group_count
    members = lax.axis_size("inner")
    teams = lax.axis_size("outer")
    owned = width // members
    shape = jax.ShapeDtypeStruct
    sems = pltpu.SemaphoreType.DMA

    product = (key_mr.astype(F32) * value_mr.astype(F32)).astype(BF16)
    rim = from_behind(product, AXES, 1)

    backward = (LANES - jnp.arange(LANES)) % LANES
    taps = mr_filter.astype(F32)
    taps = jnp.concatenate([taps[:1], taps[:0:-1]], axis=0).T
    scaled = residue * jnp.sqrt(-jnp.expm1(-2.0 * pole_rate))
    rate_t = pole_rate.T
    long_taps = jnp.sum(
        scaled.T[:, :, None] * jnp.exp(-rate_t[:, :, None] * backward.astype(F32)[None, None, :]), axis=1
    )
    position = jnp.arange(rows, dtype=F32)
    flat_rate = rate_t.reshape(-1)
    ending = jnp.exp(-flat_rate[:, None] * (rows - 1.0 - position)[None, :]).astype(BF16)
    entering = (jnp.exp(-flat_rate[None, :] * (position + 1.0)[:, None]) * scaled.T.reshape(1, -1)).astype(BF16)
    own_groups = owned // per_group
    own_rate = lax.dynamic_slice_in_dim(pole_rate, lax.axis_index("inner") * own_groups, own_groups, 1)
    own_rate = jnp.repeat(own_rate, per_group, axis=1)
    decay = jnp.exp(-own_rate * rows)
    team_decay = jnp.exp(-own_rate * (rows * members))

    full = shape((rows, width), BF16)
    block = pltpu.VMEM((rows, width), BF16)
    table = shape((width // LANES, LANES // per_group * SUB, LANES + SUB), BF16)
    table_block = pltpu.VMEM(table.shape, BF16)
    medium_table, long_table = call(
        functools.partial(table_kernel, per_group),
        (table, table),
        [VMEM, VMEM],
        (HBM, HBM),
        "tables",
        (table_block, table_block, sems((2,))),
        0,
        16 * rows * width,
    )(taps, long_taps)

    mixed_mr, gated, states = call(
        functools.partial(medium_kernel, per_group),
        (full, full, shape((members, poles, owned), BF16)),
        [HBM] * 9,
        (HBM, HBM, VMEM),
        "medium",
        (table_block,)
        + (block,) * 5
        + (pltpu.VMEM((width, rows), BF16),)
        + (block,) * 2
        + (pltpu.VMEM((rows, LANES), F32), sems((PARTS, 5)), sems((2,)), sems((2, PARTS))),
        16 * rows * rows * width,
        14 * rows * width,
    )(medium_table, rim, product, query_mr, resid, key_li, ending, long_table, entering)

    states = lax.all_to_all(states, "inner", 0, 0, tiled=True)
    total = call(total_kernel, shape((teams, poles, owned), BF16), [VMEM, VMEM], VMEM, "total", limit=SMALL)(
        states, decay
    )
    totals = lax.all_to_all(total, "outer", 0, 0, tiled=True)
    local, token = call(
        functools.partial(local_kernel, per_group),
        (shape((rows, width), F32), shape((8, LANES), F32)),
        [HBM, HBM, HBM],
        (HBM, VMEM),
        "local",
        (table_block, block, pltpu.VMEM((rows, width), F32), sems((PARTS, 2)), sems((PARTS,))),
        16 * rows * rows * width,
        14 * rows * width,
    )(long_table, gated, total)
    entered = call(
        enter_kernel,
        shape((members, poles, owned), BF16),
        [SMEM] + [VMEM] * 5,
        VMEM,
        "enter",
        limit=SMALL,
    )(lax.axis_index("outer").astype(jnp.int32).reshape(1), states, totals, decay, team_decay, token)
    entered = lax.all_to_all(entered, "inner", 0, 0, tiled=True)

    long_out = call(
        functools.partial(final_kernel, per_group),
        full,
        [HBM, VMEM, HBM, HBM],
        HBM,
        "final",
        (block, pltpu.VMEM((rows, width), F32), block, block, sems((PARTS, 3)), sems((PARTS,))),
    )(entering, entered, local, query_li)
    return (mixed_mr, long_out)


def solution(mesh):
    rows = P(AXES, None)
    return jax.shard_map(
        shards,
        mesh=mesh,
        in_specs=(rows,) * 6 + (P(), P(), P()),
        out_specs=(rows, rows),
        check_vma=False,
    )
```

```python
import functools

import jax
import jax.numpy as jnp
from jax import lax
from jax.experimental import pallas as pl
from jax.experimental.pallas import tpu as pltpu
from jax.sharding import PartitionSpec as P

EPSILON = 1e-06
AXES = ("outer", "inner")
LANES = 128
HALF = LANES // 2
SUB = 32
PARTS = 4
MIB = 1024 * 1024
F32 = jnp.float32
BF16 = jnp.bfloat16
VMEM = pl.BlockSpec(memory_space=pltpu.VMEM)
HBM = pl.BlockSpec(memory_space=pltpu.HBM)
SMEM = pl.BlockSpec(memory_space=pltpu.SMEM)


def from_behind(block, axis, distance):
    devices = range(lax.axis_size(axis))
    route = [(i - distance, i) for i in devices if i - distance in devices]
    return lax.ppermute(block, axis, route)


def span(index, size):
    return pl.ds(pl.multiple_of(index * size, size), size)


def own_lanes(stack, rows, groups, per_group):
    group = lax.broadcasted_iota(jnp.int32, (rows, LANES), 1) % (groups * per_group) // per_group
    out = stack[:rows]
    for g in range(1, groups):
        out = jnp.where(group == g, stack[g * rows : (g + 1) * rows], out)
    return out


def half_turn(block):
    return jnp.concatenate([block[:, HALF:], block[:, :HALF]], axis=1)


def causal(table, old, new, per_group):
    rows = new.shape[0]

    def window(before, now, b):
        return jnp.concatenate([before[b * SUB :], now[: (b + 1) * SUB]], axis=0)

    old_turned, new_turned = half_turn(old), half_turn(new)
    depth = rows + SUB
    low = lax.broadcasted_iota(jnp.int32, (depth, LANES), 1) < HALF
    first, second = [], []
    for b in range(0, rows // SUB, 2):
        straight, turned = window(old, new, b), window(old_turned, new_turned, b + 1)
        first.append(jnp.where(low, straight, turned))
        second.append(jnp.where(low, turned, straight))
    middle = table.shape[0] // 2
    stack_a = jnp.dot(table[:middle], jnp.concatenate(first, axis=1), preferred_element_type=F32)
    stack_b = jnp.dot(table[middle:], jnp.concatenate(second, axis=1), preferred_element_type=F32)
    low = lax.broadcasted_iota(jnp.int32, (SUB, LANES), 1) < HALF
    out = []
    for j in range(rows // SUB // 2):
        cols = slice(j * LANES, (j + 1) * LANES)
        a = own_lanes(stack_a[:, cols], SUB, HALF // per_group, per_group)
        b = own_lanes(stack_b[:, cols], SUB, HALF // per_group, per_group)
        out.append(jnp.where(low, a, b))
        out.append(pltpu.roll(jnp.where(low, b, a), HALF, 1))
    return out


def table_kernel(per_group, medium_taps_ref, long_taps_ref, medium_hbm, long_hbm, medium_ref, long_ref, sems):
    groups = LANES // per_group
    slabs = medium_ref.shape[0]
    row = lax.broadcasted_iota(jnp.int32, (SUB, LANES), 0)
    lane = lax.broadcasted_iota(jnp.int32, (SUB, LANES), 1)
    copies = []
    for i, (taps_ref, table_ref, out_hbm) in enumerate(
        ((medium_taps_ref, medium_ref, medium_hbm), (long_taps_ref, long_ref, long_hbm))
    ):

        def fill(slab, _):
            taps = taps_ref[span(slab, groups), :]
            for g in range(groups):
                turned = pltpu.roll(jnp.broadcast_to(taps[g : g + 1, :], (SUB, LANES)), 0, 1, stride=1, stride_axis=0)
                rows = slice(g * SUB, (g + 1) * SUB)
                table_ref[slab, rows, :LANES] = jnp.where(lane > row, turned, 0.0).astype(BF16)
                table_ref[slab, rows, LANES:] = jnp.where(lane <= row, turned, 0.0)[:, :SUB].astype(BF16)
            return 0

        lax.fori_loop(0, slabs, fill, 0, unroll=4)
        copies.append(pltpu.make_async_copy(table_ref, out_hbm, sems.at[i]))
        copies[i].start()
    for copy in copies:
        copy.wait()


def medium_kernel(per_group, table_hbm, rim_hbm, product_hbm, query_hbm, resid_hbm, key_hbm, ending_hbm, long_hbm,
                  entering_hbm, mixed_hbm, gated_hbm, state_ref, table_ref, rim_ref, product_ref, query_ref, resid_ref,
                  key_ref, ending_ref, mixed_ref, gated_ref, square_ref, load_sems, late_sems, store_sems):
    rows, width = product_ref.shape
    slabs = width // LANES // PARTS

    def loads(part):
        cols = span(part, width // PARTS)
        several = pl.ds(part * slabs, slabs)
        pairs = [(table_hbm.at[several], table_ref.at[several])]
        pairs += [
            (source.at[:, cols], target.at[:, cols])
            for source, target in (
                (rim_hbm, rim_ref), (product_hbm, product_ref), (query_hbm, query_ref), (resid_hbm, resid_ref)
            )
        ]
        return [pltpu.make_async_copy(*pair, load_sems.at[part, i]) for i, pair in enumerate(pairs)]

    def store(source, target, part, which):
        cols = span(part, width // PARTS)
        return pltpu.make_async_copy(source.at[:, cols], target.at[:, cols], store_sems.at[which, part])

    late = [
        pltpu.make_async_copy(key_hbm, key_ref, late_sems.at[0]),
        pltpu.make_async_copy(ending_hbm, ending_ref, late_sems.at[1]),
    ]
    for part in range(PARTS):
        for copy in loads(part):
            copy.start()
    for copy in late:
        copy.start()
    square_ref[...] = jnp.zeros_like(square_ref)

    def mix(part, _):
        for copy in loads(part):
            copy.wait()

        def one(turn, _):
            slab = part * slabs + turn
            cols = span(slab, LANES)
            convolved = causal(table_ref[slab], rim_ref[:, cols], product_ref[:, cols], per_group)
            for b, sums in enumerate(convolved):
                block = slice(b * SUB, (b + 1) * SUB)
                mixed = (resid_ref[block, cols].astype(F32) + query_ref[block, cols].astype(F32) * sums).astype(BF16)
                mixed_ref[block, cols] = mixed
                stream = mixed.astype(F32)
                square_ref[block, :] += stream * stream
            return 0

        lax.fori_loop(0, slabs, one, 0, unroll=True)
        store(mixed_ref, mixed_hbm, part, 0).start()
        return 0

    lax.fori_loop(0, PARTS, mix, 0)
    mean = jnp.sum(square_ref[...], axis=1, keepdims=True) * (1.0 / width)
    square_ref[...] = jnp.broadcast_to(lax.rsqrt(mean + EPSILON), square_ref.shape)
    owners, poles, owned = state_ref.shape
    for copy in late:
        copy.wait()

    def gate(part, _):
        def one(turn, _):
            slab = part * slabs + turn
            cols = span(slab, LANES)
            gated = (key_ref[:, cols].astype(F32) * mixed_ref[:, cols].astype(F32) * square_ref[...]).astype(BF16)
            gated_ref[:, cols] = gated
            stack = jnp.dot(ending_ref[cols, :], gated, preferred_element_type=F32)
            state_ref[slab] = own_lanes(stack, poles, LANES // per_group, per_group).astype(BF16)
            return 0

        lax.fori_loop(0, slabs, one, 0, unroll=True)
        store(gated_ref, gated_hbm, part, 1).start()
        return 0

    lax.fori_loop(0, PARTS, gate, 0)
    for part in range(PARTS):
        store(mixed_ref, mixed_hbm, part, 0).wait()
        store(gated_ref, gated_hbm, part, 1).wait()


def local_kernel(per_group, table_hbm, gated_hbm, after_ref, local_hbm, token_ref, table_ref, gated_ref, local_ref,
                 load_sems, store_sems):
    rows, width = gated_ref.shape
    slabs = width // LANES // PARTS

    def loads(part):
        cols = span(part, width // PARTS)
        several = pl.ds(part * slabs, slabs)
        return [
            pltpu.make_async_copy(table_hbm.at[several], table_ref.at[several], load_sems.at[part, 0]),
            pltpu.make_async_copy(gated_hbm.at[:, cols], gated_ref.at[:, cols], load_sems.at[part, 1]),
        ]

    def store(part):
        cols = span(part, width // PARTS)
        return pltpu.make_async_copy(local_ref.at[:, cols], local_hbm.at[:, cols], store_sems.at[part])

    for part in range(PARTS):
        for copy in loads(part):
            copy.start()
    token_ref[...] = jnp.zeros_like(token_ref)

    def convolve(part, _):
        for copy in loads(part):
            copy.wait()

        def one(turn, _):
            slab = part * slabs + turn
            cols = span(slab, LANES)
            old = jnp.zeros((rows, LANES), BF16)
            for b, sums in enumerate(causal(table_ref[slab], old, gated_ref[:, cols], per_group)):
                local_ref[b * SUB : (b + 1) * SUB, cols] = sums
            return 0

        lax.fori_loop(0, slabs, one, 0, unroll=True)
        store(part).start()
        return 0

    lax.fori_loop(0, PARTS, convolve, 0)
    for part in range(PARTS):
        store(part).wait()


def total_kernel(states_ref, decay_ref, total_ref):
    decay = decay_ref[...]
    total = states_ref[0].astype(F32)
    for i in range(1, states_ref.shape[0]):
        total = decay * total + states_ref[i].astype(F32)
    total = total.astype(BF16)
    for i in range(total_ref.shape[0]):
        total_ref[i] = total


def enter_kernel(place_ref, states_ref, totals_ref, decay_ref, group_decay_ref, after_ref, entered_ref):
    place = place_ref[0]
    group_decay = group_decay_ref[...]

    def one(turn, state):
        return group_decay * state + totals_ref[turn].astype(F32)

    state = lax.fori_loop(0, place, one, jnp.zeros_like(group_decay))
    decay = decay_ref[...]
    for i in range(states_ref.shape[0]):
        entered_ref[i] = state.astype(BF16)
        if i + 1 < states_ref.shape[0]:
            state = decay * state + states_ref[i].astype(F32)


def final_kernel(per_group, entering_hbm, state_ref, local_hbm, query_hbm, out_hbm,
                 entering_ref, local_ref, query_ref, out_ref, load_sems, store_sems):
    owners, poles, owned = state_ref.shape
    width = owners * owned
    pair = 2
    steps = owners // pair // PARTS

    def loads(part):
        cols = span(part, width // PARTS)
        pairs = ((entering_hbm, entering_ref), (local_hbm, local_ref), (query_hbm, query_ref))
        return [
            pltpu.make_async_copy(source.at[:, cols], target.at[:, cols], load_sems.at[part, i])
            for i, (source, target) in enumerate(pairs)
        ]

    def store(part):
        cols = span(part, width // PARTS)
        return pltpu.make_async_copy(out_ref.at[:, cols], out_hbm.at[:, cols], store_sems.at[part])

    for part in range(PARTS):
        for copy in loads(part):
            copy.start()
    spread = pair * owned // per_group
    row_group = lax.broadcasted_iota(jnp.int32, (spread * poles, pair * owned), 0) // poles
    lane_group = lax.broadcasted_iota(jnp.int32, (spread * poles, pair * owned), 1) // per_group
    own = row_group == lane_group

    def finish(part, _):
        for copy in loads(part):
            copy.wait()

        def one(turn, _):
            slab = part * steps + turn
            cols = span(slab, pair * owned)
            state = jnp.concatenate([state_ref[slab * pair + i] for i in range(pair)], axis=1)
            diagonal = jnp.where(own, jnp.concatenate([state] * spread, axis=0), jnp.zeros((), BF16))
            carried = jnp.dot(entering_ref[:, cols], diagonal, preferred_element_type=F32)
            out_ref[:, cols] = (query_ref[:, cols].astype(F32) * (local_ref[:, cols] + carried)).astype(BF16)
            return 0

        lax.fori_loop(0, steps, one, 0, unroll=True)
        store(part).start()
        return 0

    lax.fori_loop(0, PARTS, finish, 0)
    for part in range(PARTS):
        store(part).wait()


def call(body, out, in_specs, out_specs, name, scratch=(), flops=0, moved=0, limit=50 * MIB):
    return pl.pallas_call(
        body,
        out_shape=out,
        in_specs=in_specs,
        out_specs=out_specs,
        scratch_shapes=scratch,
        name=name,
        cost_estimate=pl.CostEstimate(flops=flops, bytes_accessed=moved, transcendentals=0),
        compiler_params=pltpu.CompilerParams(vmem_limit_bytes=limit),
    )


def shards(resid, query_mr, key_mr, value_mr, query_li, key_li, mr_filter, pole_rate, residue):
    tap_count, group_count = mr_filter.shape
    poles = pole_rate.shape[0]
    rows, width = resid.shape
    per_group = width // group_count
    members = lax.axis_size("inner")
    teams = lax.axis_size("outer")
    owned = width // members
    shape = jax.ShapeDtypeStruct
    sems = pltpu.SemaphoreType.DMA

    product = (key_mr.astype(F32) * value_mr.astype(F32)).astype(BF16)
    rim = from_behind(product, AXES, 1)

    backward = (LANES - jnp.arange(LANES)) % LANES
    taps = mr_filter.astype(F32)
    taps = jnp.concatenate([taps[:1], taps[:0:-1]], axis=0).T
    scaled = residue * jnp.sqrt(-jnp.expm1(-2.0 * pole_rate))
    rate_t = pole_rate.T
    long_taps = jnp.sum(
        scaled.T[:, :, None] * jnp.exp(-rate_t[:, :, None] * backward.astype(F32)[None, None, :]), axis=1
    )
    position = jnp.arange(rows, dtype=F32)
    flat_rate = rate_t.reshape(-1)
    ending = jnp.exp(-flat_rate[:, None] * (rows - 1.0 - position)[None, :]).astype(BF16)
    entering = (jnp.exp(-flat_rate[None, :] * (position + 1.0)[:, None]) * scaled.T.reshape(1, -1)).astype(BF16)
    own_groups = owned // per_group
    own_rate = lax.dynamic_slice_in_dim(pole_rate, lax.axis_index("inner") * own_groups, own_groups, 1)
    own_rate = jnp.repeat(own_rate, per_group, axis=1)
    decay = jnp.exp(-own_rate * rows)
    team_decay = jnp.exp(-own_rate * (rows * members))

    full = shape((rows, width), BF16)
    block = pltpu.VMEM((rows, width), BF16)
    table = shape((width // LANES, LANES // per_group * SUB, LANES + SUB), BF16)
    table_block = pltpu.VMEM(table.shape, BF16)
    medium_table, long_table = call(
        functools.partial(table_kernel, per_group),
        (table, table),
        [VMEM, VMEM],
        (HBM, HBM),
        "tables",
        (table_block, table_block, sems((2,))),
        0,
        16 * rows * width,
        12 * MIB,
    )(taps, long_taps)

    mixed_mr, gated, states = call(
        functools.partial(medium_kernel, per_group),
        (full, full, shape((members, poles, owned), BF16)),
        [HBM] * 9,
        (HBM, HBM, VMEM),
        "medium",
        (table_block,)
        + (block,) * 5
        + (pltpu.VMEM((width, rows), BF16),)
        + (block,) * 2
        + (pltpu.VMEM((rows, LANES), F32), sems((PARTS, 5)), sems((2,)), sems((2, PARTS))),
        16 * rows * rows * width,
        14 * rows * width,
    )(medium_table, rim, product, query_mr, resid, key_li, ending, long_table, entering)

    states = lax.all_to_all(states, "inner", 0, 0, tiled=True)
    total = call(total_kernel, shape((teams, poles, owned), BF16), [VMEM, VMEM], VMEM, "total", limit=4 * MIB)(
        states, decay
    )
    totals = lax.all_to_all(total, "outer", 0, 0, tiled=True)
    local, token = call(
        functools.partial(local_kernel, per_group),
        (shape((rows, width), F32), shape((8, LANES), F32)),
        [HBM, HBM, HBM],
        (HBM, VMEM),
        "local",
        (table_block, block, pltpu.VMEM((rows, width), F32), sems((PARTS, 2)), sems((PARTS,))),
        16 * rows * rows * width,
        14 * rows * width,
    )(long_table, gated, total)
    entered = call(
        enter_kernel,
        shape((members, poles, owned), BF16),
        [SMEM] + [VMEM] * 5,
        VMEM,
        "enter",
        limit=4 * MIB,
    )(lax.axis_index("outer").astype(jnp.int32).reshape(1), states, totals, decay, team_decay, token)
    entered = lax.all_to_all(entered, "inner", 0, 0, tiled=True)

    long_out = call(
        functools.partial(final_kernel, per_group),
        full,
        [HBM, VMEM, HBM, HBM],
        HBM,
        "final",
        (block, pltpu.VMEM((rows, width), F32), block, block, sems((PARTS, 3)), sems((PARTS,))),
    )(entering, entered, local, query_li)
    return (mixed_mr, long_out)


def solution(mesh):
    rows = P(AXES, None)
    return jax.shard_map(
        shards,
        mesh=mesh,
        in_specs=(rows,) * 6 + (P(), P(), P()),
        out_specs=(rows, rows),
        check_vma=False,
    )
```

```python
import functools

import jax
import jax.numpy as jnp
from jax import lax
from jax.experimental import pallas as pl
from jax.experimental.pallas import tpu as pltpu
from jax.sharding import PartitionSpec as P

EPSILON = 1e-06
AXES = ("outer", "inner")
LANES = 128
HALF = LANES // 2
SUB = 32
PARTS = 4
MIB = 1024 * 1024
F32 = jnp.float32
BF16 = jnp.bfloat16
VMEM = pl.BlockSpec(memory_space=pltpu.VMEM)
HBM = pl.BlockSpec(memory_space=pltpu.HBM)
SMEM = pl.BlockSpec(memory_space=pltpu.SMEM)


def from_behind(block, axis, distance):
    devices = range(lax.axis_size(axis))
    route = [(i - distance, i) for i in devices if i - distance in devices]
    return lax.ppermute(block, axis, route)


def span(index, size):
    return pl.ds(pl.multiple_of(index * size, size), size)


def own_lanes(stack, rows, groups, per_group):
    group = lax.broadcasted_iota(jnp.int32, (rows, LANES), 1) % (groups * per_group) // per_group
    out = stack[:rows]
    for g in range(1, groups):
        out = jnp.where(group == g, stack[g * rows : (g + 1) * rows], out)
    return out


def half_turn(block):
    return jnp.concatenate([block[:, HALF:], block[:, :HALF]], axis=1)


def causal(table, old, new, per_group):
    rows = new.shape[0]

    def window(before, now, b):
        return jnp.concatenate([before[b * SUB :], now[: (b + 1) * SUB]], axis=0)

    old_turned, new_turned = half_turn(old), half_turn(new)
    depth = rows + SUB
    low = lax.broadcasted_iota(jnp.int32, (depth, LANES), 1) < HALF
    first, second = [], []
    for b in range(0, rows // SUB, 2):
        straight, turned = window(old, new, b), window(old_turned, new_turned, b + 1)
        first.append(jnp.where(low, straight, turned))
        second.append(jnp.where(low, turned, straight))
    middle = table.shape[0] // 2
    stack_a = jnp.dot(table[:middle], jnp.concatenate(first, axis=1), preferred_element_type=F32)
    stack_b = jnp.dot(table[middle:], jnp.concatenate(second, axis=1), preferred_element_type=F32)
    low = lax.broadcasted_iota(jnp.int32, (SUB, LANES), 1) < HALF
    out = []
    for j in range(rows // SUB // 2):
        cols = slice(j * LANES, (j + 1) * LANES)
        a = own_lanes(stack_a[:, cols], SUB, HALF // per_group, per_group)
        b = own_lanes(stack_b[:, cols], SUB, HALF // per_group, per_group)
        out.append(jnp.where(low, a, b))
        out.append(pltpu.roll(jnp.where(low, b, a), HALF, 1))
    return out


def table_kernel(per_group, medium_taps_ref, long_taps_ref, medium_hbm, long_hbm, medium_ref, long_ref, sems):
    groups = LANES // per_group
    slabs = medium_ref.shape[0]
    row = lax.broadcasted_iota(jnp.int32, (SUB, LANES), 0)
    lane = lax.broadcasted_iota(jnp.int32, (SUB, LANES), 1)
    copies = []
    for i, (taps_ref, table_ref, out_hbm) in enumerate(
        ((medium_taps_ref, medium_ref, medium_hbm), (long_taps_ref, long_ref, long_hbm))
    ):

        def fill(slab, _):
            taps = taps_ref[span(slab, groups), :]
            for g in range(groups):
                turned = pltpu.roll(jnp.broadcast_to(taps[g : g + 1, :], (SUB, LANES)), 0, 1, stride=1, stride_axis=0)
                rows = slice(g * SUB, (g + 1) * SUB)
                table_ref[slab, rows, :LANES] = jnp.where(lane > row, turned, 0.0).astype(BF16)
                table_ref[slab, rows, LANES:] = jnp.where(lane <= row, turned, 0.0)[:, :SUB].astype(BF16)
            return 0

        lax.fori_loop(0, slabs, fill, 0, unroll=4)
        copies.append(pltpu.make_async_copy(table_ref, out_hbm, sems.at[i]))
        copies[i].start()
    for copy in copies:
        copy.wait()


def medium_kernel(per_group, table_hbm, rim_ref, product_ref, query_hbm, resid_hbm, key_hbm, ending_hbm, long_hbm,
                  entering_hbm, mixed_hbm, gated_hbm, state_ref, table_ref, query_ref, resid_ref,
                  key_ref, ending_ref, mixed_ref, gated_ref, square_ref, load_sems, late_sems, store_sems):
    rows, width = product_ref.shape
    slabs = width // LANES // PARTS

    def loads(part):
        cols = span(part, width // PARTS)
        several = pl.ds(part * slabs, slabs)
        pairs = [(table_hbm.at[several], table_ref.at[several])]
        pairs += [
            (source.at[:, cols], target.at[:, cols])
            for source, target in ((query_hbm, query_ref), (resid_hbm, resid_ref))
        ]
        return [pltpu.make_async_copy(*pair, load_sems.at[part, i]) for i, pair in enumerate(pairs)]

    def store(source, target, part, which):
        cols = span(part, width // PARTS)
        return pltpu.make_async_copy(source.at[:, cols], target.at[:, cols], store_sems.at[which, part])

    late = [
        pltpu.make_async_copy(key_hbm, key_ref, late_sems.at[0]),
        pltpu.make_async_copy(ending_hbm, ending_ref, late_sems.at[1]),
    ]
    for part in range(PARTS):
        for copy in loads(part):
            copy.start()
    for copy in late:
        copy.start()
    square_ref[...] = jnp.zeros_like(square_ref)

    def mix(part, _):
        for copy in loads(part):
            copy.wait()

        def one(turn, _):
            slab = part * slabs + turn
            cols = span(slab, LANES)
            convolved = causal(table_ref[slab], rim_ref[:, cols], product_ref[:, cols], per_group)
            for b, sums in enumerate(convolved):
                block = slice(b * SUB, (b + 1) * SUB)
                mixed = (resid_ref[block, cols].astype(F32) + query_ref[block, cols].astype(F32) * sums).astype(BF16)
                mixed_ref[block, cols] = mixed
                stream = mixed.astype(F32)
                square_ref[block, :] += stream * stream
            return 0

        lax.fori_loop(0, slabs, one, 0, unroll=True)
        store(mixed_ref, mixed_hbm, part, 0).start()
        return 0

    lax.fori_loop(0, PARTS, mix, 0)
    mean = jnp.sum(square_ref[...], axis=1, keepdims=True) * (1.0 / width)
    square_ref[...] = jnp.broadcast_to(lax.rsqrt(mean + EPSILON), square_ref.shape)
    owners, poles, owned = state_ref.shape
    for copy in late:
        copy.wait()

    def gate(part, _):
        def one(turn, _):
            slab = part * slabs + turn
            cols = span(slab, LANES)
            gated = (key_ref[:, cols].astype(F32) * mixed_ref[:, cols].astype(F32) * square_ref[...]).astype(BF16)
            gated_ref[:, cols] = gated
            stack = jnp.dot(ending_ref[cols, :], gated, preferred_element_type=F32)
            state_ref[slab] = own_lanes(stack, poles, LANES // per_group, per_group).astype(BF16)
            return 0

        lax.fori_loop(0, slabs, one, 0, unroll=True)
        store(gated_ref, gated_hbm, part, 1).start()
        return 0

    lax.fori_loop(0, PARTS, gate, 0)
    for part in range(PARTS):
        store(mixed_ref, mixed_hbm, part, 0).wait()
        store(gated_ref, gated_hbm, part, 1).wait()


def local_kernel(per_group, table_hbm, gated_ref, after_ref, local_hbm, token_ref, table_ref, local_ref,
                 load_sems, store_sems):
    rows, width = gated_ref.shape
    slabs = width // LANES // PARTS

    def loads(part):
        several = pl.ds(part * slabs, slabs)
        return [
            pltpu.make_async_copy(table_hbm.at[several], table_ref.at[several], load_sems.at[part, 0]),
        ]

    def store(part):
        cols = span(part, width // PARTS)
        return pltpu.make_async_copy(local_ref.at[:, cols], local_hbm.at[:, cols], store_sems.at[part])

    for part in range(PARTS):
        for copy in loads(part):
            copy.start()
    token_ref[...] = jnp.zeros_like(token_ref)

    def convolve(part, _):
        for copy in loads(part):
            copy.wait()

        def one(turn, _):
            slab = part * slabs + turn
            cols = span(slab, LANES)
            old = jnp.zeros((rows, LANES), BF16)
            for b, sums in enumerate(causal(table_ref[slab], old, gated_ref[:, cols], per_group)):
                local_ref[b * SUB : (b + 1) * SUB, cols] = sums
            return 0

        lax.fori_loop(0, slabs, one, 0, unroll=True)
        store(part).start()
        return 0

    lax.fori_loop(0, PARTS, convolve, 0)
    for part in range(PARTS):
        store(part).wait()


def total_kernel(states_ref, decay_ref, total_ref):
    decay = decay_ref[...]
    total = states_ref[0].astype(F32)
    for i in range(1, states_ref.shape[0]):
        total = decay * total + states_ref[i].astype(F32)
    total = total.astype(BF16)
    for i in range(total_ref.shape[0]):
        total_ref[i] = total


def enter_kernel(place_ref, states_ref, totals_ref, decay_ref, group_decay_ref, after_ref, entered_ref):
    place = place_ref[0]
    group_decay = group_decay_ref[...]

    def one(turn, state):
        return group_decay * state + totals_ref[turn].astype(F32)

    state = lax.fori_loop(0, place, one, jnp.zeros_like(group_decay))
    decay = decay_ref[...]
    for i in range(states_ref.shape[0]):
        entered_ref[i] = state.astype(BF16)
        if i + 1 < states_ref.shape[0]:
            state = decay * state + states_ref[i].astype(F32)


def final_kernel(per_group, entering_ref, state_ref, local_hbm, query_ref, out_hbm,
                 local_ref, out_ref, load_sems, store_sems):
    owners, poles, owned = state_ref.shape
    width = owners * owned
    pair = 2
    steps = owners // pair // PARTS

    def loads(part):
        cols = span(part, width // PARTS)
        pairs = ((local_hbm, local_ref),)
        return [
            pltpu.make_async_copy(source.at[:, cols], target.at[:, cols], load_sems.at[part, i])
            for i, (source, target) in enumerate(pairs)
        ]

    def store(part):
        cols = span(part, width // PARTS)
        return pltpu.make_async_copy(out_ref.at[:, cols], out_hbm.at[:, cols], store_sems.at[part])

    for part in range(PARTS):
        for copy in loads(part):
            copy.start()
    spread = pair * owned // per_group
    row_group = lax.broadcasted_iota(jnp.int32, (spread * poles, pair * owned), 0) // poles
    lane_group = lax.broadcasted_iota(jnp.int32, (spread * poles, pair * owned), 1) // per_group
    own = row_group == lane_group

    def finish(part, _):
        for copy in loads(part):
            copy.wait()

        def one(turn, _):
            slab = part * steps + turn
            cols = span(slab, pair * owned)
            state = jnp.concatenate([state_ref[slab * pair + i] for i in range(pair)], axis=1)
            diagonal = jnp.where(own, jnp.concatenate([state] * spread, axis=0), jnp.zeros((), BF16))
            carried = jnp.dot(entering_ref[:, cols], diagonal, preferred_element_type=F32)
            out_ref[:, cols] = (query_ref[:, cols].astype(F32) * (local_ref[:, cols] + carried)).astype(BF16)
            return 0

        lax.fori_loop(0, steps, one, 0, unroll=True)
        store(part).start()
        return 0

    lax.fori_loop(0, PARTS, finish, 0)
    for part in range(PARTS):
        store(part).wait()


def call(body, out, in_specs, out_specs, name, scratch=(), flops=0, moved=0, limit=50 * MIB):
    return pl.pallas_call(
        body,
        out_shape=out,
        in_specs=in_specs,
        out_specs=out_specs,
        scratch_shapes=scratch,
        name=name,
        cost_estimate=pl.CostEstimate(flops=flops, bytes_accessed=moved, transcendentals=0),
        compiler_params=pltpu.CompilerParams(vmem_limit_bytes=limit),
    )


def shards(resid, query_mr, key_mr, value_mr, query_li, key_li, mr_filter, pole_rate, residue):
    tap_count, group_count = mr_filter.shape
    poles = pole_rate.shape[0]
    rows, width = resid.shape
    per_group = width // group_count
    members = lax.axis_size("inner")
    teams = lax.axis_size("outer")
    owned = width // members
    shape = jax.ShapeDtypeStruct
    sems = pltpu.SemaphoreType.DMA

    product = (key_mr.astype(F32) * value_mr.astype(F32)).astype(BF16)
    rim = from_behind(product, AXES, 1)

    backward = (LANES - jnp.arange(LANES)) % LANES
    taps = mr_filter.astype(F32)
    taps = jnp.concatenate([taps[:1], taps[:0:-1]], axis=0).T
    scaled = residue * jnp.sqrt(-jnp.expm1(-2.0 * pole_rate))
    rate_t = pole_rate.T
    long_taps = jnp.sum(
        scaled.T[:, :, None] * jnp.exp(-rate_t[:, :, None] * backward.astype(F32)[None, None, :]), axis=1
    )
    position = jnp.arange(rows, dtype=F32)
    flat_rate = rate_t.reshape(-1)
    ending = jnp.exp(-flat_rate[:, None] * (rows - 1.0 - position)[None, :]).astype(BF16)
    entering = (jnp.exp(-flat_rate[None, :] * (position + 1.0)[:, None]) * scaled.T.reshape(1, -1)).astype(BF16)
    own_groups = owned // per_group
    own_rate = lax.dynamic_slice_in_dim(pole_rate, lax.axis_index("inner") * own_groups, own_groups, 1)
    own_rate = jnp.repeat(own_rate, per_group, axis=1)
    decay = jnp.exp(-own_rate * rows)
    team_decay = jnp.exp(-own_rate * (rows * members))

    full = shape((rows, width), BF16)
    block = pltpu.VMEM((rows, width), BF16)
    table = shape((width // LANES, LANES // per_group * SUB, LANES + SUB), BF16)
    table_block = pltpu.VMEM(table.shape, BF16)
    medium_table, long_table = call(
        functools.partial(table_kernel, per_group),
        (table, table),
        [VMEM, VMEM],
        (HBM, HBM),
        "tables",
        (table_block, table_block, sems((2,))),
        0,
        16 * rows * width,
        12 * MIB,
    )(taps, long_taps)

    mixed_mr, gated, states = call(
        functools.partial(medium_kernel, per_group),
        (full, full, shape((members, poles, owned), BF16)),
        [HBM, VMEM, VMEM] + [HBM] * 6,
        (HBM, HBM, VMEM),
        "medium",
        (table_block,)
        + (block,) * 3
        + (pltpu.VMEM((width, rows), BF16),)
        + (block,) * 2
        + (pltpu.VMEM((rows, LANES), F32), sems((PARTS, 3)), sems((2,)), sems((2, PARTS))),
        16 * rows * rows * width,
        14 * rows * width,
    )(medium_table, rim, product, query_mr, resid, key_li, ending, long_table, entering)

    states = lax.all_to_all(states, "inner", 0, 0, tiled=True)
    total = call(total_kernel, shape((teams, poles, owned), BF16), [VMEM, VMEM], VMEM, "total", limit=4 * MIB)(
        states, decay
    )
    totals = lax.all_to_all(total, "outer", 0, 0, tiled=True)
    local, token = call(
        functools.partial(local_kernel, per_group),
        (shape((rows, width), F32), shape((8, LANES), F32)),
        [HBM, VMEM, HBM],
        (HBM, VMEM),
        "local",
        (table_block, pltpu.VMEM((rows, width), F32), sems((PARTS, 2)), sems((PARTS,))),
        16 * rows * rows * width,
        14 * rows * width,
    )(long_table, gated, total)
    entered = call(
        enter_kernel,
        shape((members, poles, owned), BF16),
        [SMEM] + [VMEM] * 5,
        VMEM,
        "enter",
        limit=4 * MIB,
    )(lax.axis_index("outer").astype(jnp.int32).reshape(1), states, totals, decay, team_decay, token)
    entered = lax.all_to_all(entered, "inner", 0, 0, tiled=True)

    long_out = call(
        functools.partial(final_kernel, per_group),
        full,
        [VMEM, VMEM, HBM, VMEM],
        HBM,
        "final",
        (pltpu.VMEM((rows, width), F32), block, sems((PARTS, 1)), sems((PARTS,))),
    )(entering, entered, local, query_li)
    return (mixed_mr, long_out)


def solution(mesh):
    rows = P(AXES, None)
    return jax.shard_map(
        shards,
        mesh=mesh,
        in_specs=(rows,) * 6 + (P(), P(), P()),
        out_specs=(rows, rows),
        check_vma=False,
    )
```
